32 devices in a mesh: parts: 2 (over y), dp: 8 (over z, x), tp: 2 (over core).
Axes of the slice: x: 2, y: 2, z: 4, core: 2. Of those that a mesh axis runs over, the one named last changes fastest.
Arguments:
- cache_keys: bfloat16 [256, 256, 512], P(('parts', 'dp'), None, 'tp'), parts along dimension 0, may hold values from -6 to 6
- cache_values: bfloat16 [256, 256, 512], P(('parts', 'dp'), None, 'tp'), parts along dimension 0, may hold values from -6 to 6
- lengths: int32 [256], P(('parts', 'dp')), parts along dimension 0, may hold values from 1 to 2, as said below
- move_to: int32 [256], P(('parts', 'dp')), parts along dimension 0, may hold values from 0 to 127, as said below
- queries: bfloat16 [256, 2, 4096], P(('parts', 'dp'), None, 'tp'), parts along dimension 0, may hold values from -150 to 150
- new_keys: bfloat16 [256, 2, 512], P(('parts', 'dp'), None, 'tp'), parts along dimension 0, may hold values from -8 to 8
- new_values: bfloat16 [256, 2, 512], P(('parts', 'dp'), None, 'tp'), parts along dimension 0, may hold values from -6 to 6
- out_weight: bfloat16 [4096, 5120], P('tp', 'dp'), may hold values from -0.09375 to 0.09375
Outputs:
- hidden: bfloat16 [256, 2, 5120], P(('parts', 'dp')), parts along dimension 0
The draws below stay inside these ranges and needn't reach their ends.
There are 2 independent parts, one for each index of `parts`. The reference program is written for one: setup_inputs(seed, part) draws one part's arguments, and reference() takes and returns one part's arrays. A program takes and returns all parts, laid end to end along the dimension named above; an argument that names none is the same for every part. Nothing has to cross between parts.
Inputs may be any that keep to these rules, and one draw needn't show every extreme that they name: `lengths`: at least one row has 2 blocks and at least one has 1. `move_to`: a permutation of the 128 slots (slot = group * 16 + index in the group, with 8 groups); in every group the same 7 indices leave and the others stay in place; the k-th of the leaving indices (k = 1 to 7, which index is which k is drawn) goes, at the same index, to the group 1 + (k - 1) * max(1, 1) further on, counted cyclically.
All inputs are finite; a program needn't handle non-finite values.
Results may differ from the reference program's by a relative error of at most 0.0057.
Values may be sent and summed in bfloat16 or wider, within the bound.
A program may use at most 64 MiB of HBM per device.

```python
import math
import jax
import jax.numpy as jnp
from jax import lax

D = 5120
QH = 32
KVH = 4
HD = 128
BLK = 128
MAXB = 2
STEPS = 2
ROWS = 16
SLOTS = 128
MOVES = 7


def shared_keys(key):
    return jax.random.truncated_normal(key, -6.0, 6.0, (SLOTS, STEPS, KVH * HD), jnp.float32)


def draw_new_keys(key, part):
    base_keys = shared_keys(key)
    return base_keys.astype(jnp.bfloat16)


def draw_queries(key, part):
    key = jax.random.fold_in(key, 12)
    drawn = jax.random.truncated_normal(key, -6.0, 6.0, (SLOTS, STEPS, QH * HD), jnp.float32)
    return drawn.astype(jnp.bfloat16)


def draw_lengths(key, part):
    key = jax.random.fold_in(key, 31)
    drawn = jax.random.randint(key, (SLOTS,), 1, MAXB + 1)
    return drawn.at[0].set(MAXB).at[1].set(1).astype(jnp.int32)


def draw_move_to(key, part):
    key = jax.random.fold_in(key, 21)
    group_count = SLOTS // ROWS
    stride = max(1, group_count // (MOVES + 1))
    moving_slots = jax.random.permutation(key, ROWS)[:MOVES].astype(jnp.int32)
    offsets = (1 + jnp.arange(MOVES, dtype=jnp.int32) * stride).astype(jnp.int32)
    slot_offset = jnp.zeros((ROWS,), jnp.int32).at[moving_slots].set(offsets)
    slot_ids = jnp.arange(SLOTS, dtype=jnp.int32)
    group_ids = slot_ids // ROWS
    index_ids = slot_ids % ROWS
    target_group = (group_ids + slot_offset[index_ids]) % group_count
    return (target_group * ROWS + index_ids).astype(jnp.int32)


def block_levels(stream_key, extent, pieces, least, top_value):
    gain = 1.0
    for position, blocks in pieces:
        steps = jax.random.uniform(jax.random.fold_in(jax.random.fold_in(stream_key, 6), position), (blocks,), jnp.float32, least / len(pieces), top_value / len(pieces))
        gain = gain * jnp.repeat(jnp.exp(steps), extent[position] // blocks).reshape((-1,) + (1,) * (len(extent) - 1 - position))
    return gain


def bell_draw(key, dims, width, bound, cuts=(), kind=jnp.bfloat16):
    loudness = block_levels(key, dims, cuts, -0.22, 0.18) if cuts else 1.0
    result = jax.random.normal(key, dims, jnp.float32) * width * loudness
    return jnp.minimum(jnp.maximum(result, -bound), bound).astype(kind)


def setup_inputs(seed: int = 0, part: int = 0) -> dict:
    splits = jax.random.split(jax.random.key(seed), 9)
    part_keys = jax.random.split(jax.random.fold_in(splits[8], part), 9)
    return {
        "cache_keys": bell_draw(part_keys[0], (SLOTS, MAXB * BLK, KVH * HD), 1.0, 6.0, ((0, 8), (2, 2))),
        "cache_values": bell_draw(part_keys[1], (SLOTS, MAXB * BLK, KVH * HD), 1.0, 6.0, ((0, 8), (2, 2))),
        "lengths": draw_lengths(jax.random.fold_in(jax.random.fold_in(splits[8], part), 71), part),
        "move_to": draw_move_to(jax.random.fold_in(jax.random.fold_in(splits[8], part), 71), part),
        "queries": draw_queries(jax.random.fold_in(jax.random.fold_in(splits[8], part), 71), part),
        "new_keys": draw_new_keys(jax.random.fold_in(jax.random.fold_in(splits[8], part), 71), part),
        "new_values": bell_draw(part_keys[6], (SLOTS, STEPS, KVH * HD), 1.0, 6.0, ((0, 8), (2, 2))),
        "out_weight": bell_draw(splits[7], (QH * HD, D), (QH * HD) ** -0.5, 0.09375, ((0, 2), (1, 8))),
    }


def attend_rows(packed):
    keys, values, row_lengths, queries, new_keys, new_values = packed
    row_count = keys.shape[0]
    span_len = MAXB * BLK
    group_size = QH // KVH
    score_scale = 1.0 / math.sqrt(HD)
    query = queries.astype(jnp.float32).reshape(row_count, STEPS, KVH, group_size, HD)
    key_block = keys.astype(jnp.float32).reshape(row_count, span_len, KVH, HD)
    value_block = values.astype(jnp.float32).reshape(row_count, span_len, KVH, HD)
    fresh_keys = new_keys.astype(jnp.float32).reshape(row_count, STEPS, KVH, HD)
    fresh_values = new_values.astype(jnp.float32).reshape(row_count, STEPS, KVH, HD)
    cache_scores = jnp.einsum('bskgd,bpkd->bskgp', query, key_block) * score_scale
    fresh_scores = jnp.einsum('bskgd,bukd->bskgu', query, fresh_keys) * score_scale
    visible = jnp.arange(span_len)[None, :] < (row_lengths * BLK)[:, None]
    causal = jnp.arange(STEPS)[None, :] <= jnp.arange(STEPS)[:, None]
    cache_scores = jnp.where(visible[:, None, None, None, :], cache_scores, -jnp.inf)
    fresh_scores = jnp.where(causal[None, :, None, None, :], fresh_scores, -jnp.inf)
    top_score = jnp.maximum(cache_scores.max(axis=-1), fresh_scores.max(axis=-1))[..., None]
    cache_exp = jnp.exp(cache_scores - top_score)
    fresh_exp = jnp.exp(fresh_scores - top_score)
    sum_exp = cache_exp.sum(axis=-1, keepdims=True) + fresh_exp.sum(axis=-1, keepdims=True)
    cache_weight = (cache_exp / sum_exp).astype(jnp.bfloat16)
    fresh_weight = (fresh_exp / sum_exp).astype(jnp.bfloat16)
    mixed = jnp.einsum('bskgp,bpkd->bskgd', cache_weight.astype(jnp.float32), value_block)
    mixed = mixed + jnp.einsum('bskgu,bukd->bskgd', fresh_weight.astype(jnp.float32), fresh_values)
    return mixed.astype(jnp.bfloat16).reshape(row_count, STEPS, QH * HD)

def reference(cache_keys, cache_values, lengths, move_to, queries, new_keys, new_values, out_weight):
    moved_keys = jnp.zeros_like(cache_keys).at[move_to].set(cache_keys)
    moved_values = jnp.zeros_like(cache_values).at[move_to].set(cache_values)
    moved_lengths = jnp.zeros_like(lengths).at[move_to].set(lengths)
    block_count = SLOTS // ROWS

    def split_rows(array):
        return array.reshape((block_count, ROWS) + array.shape[1:])
    attended = lax.map(attend_rows, (split_rows(moved_keys), split_rows(moved_values), split_rows(moved_lengths), split_rows(queries), split_rows(new_keys), split_rows(new_values)))
    attended = attended.reshape(SLOTS * STEPS, QH * HD)
    hidden = jnp.dot(attended, out_weight, preferred_element_type=jnp.float32)
    return hidden.astype(jnp.bfloat16).reshape(SLOTS, STEPS, D)
```

```python
import functools
import math

import jax
import jax.numpy as jnp
from jax import lax
from jax.experimental import pallas as pl
from jax.experimental.pallas import tpu as pltpu
from jax.sharding import PartitionSpec as P

KVH = 4
HD = 128
BLK = 128
STEPS = 2
PAY = 48
MESH = pl.DeviceIdType.MESH


def attend_slot(pay, keys, values, length):
    query = pay[0:32].astype(jnp.float32)
    extra = pay[32:48].astype(jnp.float32)
    row = lax.broadcasted_iota(jnp.int32, (32, HD), 0)
    first_kv = (row // 8) % 2 == 0
    zero = jnp.zeros_like(query)
    wide = jnp.concatenate(
        [jnp.where(first_kv, query, zero), jnp.where(first_kv, zero, query)], axis=1
    ).astype(jnp.bfloat16)
    scale = 1.0 / math.sqrt(HD)
    scores = (
        lax.dot_general(wide, keys, (((1,), (1,)), ((), ())), preferred_element_type=jnp.float32)
        * scale
    )
    span = lax.broadcasted_iota(jnp.int32, scores.shape, 1)
    scores = jnp.where(span < length * BLK, scores, -jnp.inf)
    step = lax.broadcasted_iota(jnp.int32, (32, 1), 0) // 16
    fresh = []
    for u in range(STEPS):
        key_u = jnp.where(first_kv, extra[2 * u : 2 * u + 1], extra[2 * u + 1 : 2 * u + 2])
        score_u = jnp.sum(query * key_u, axis=1, keepdims=True) * scale
        fresh.append(jnp.where(step >= u, score_u, -jnp.inf))
    top = jnp.max(scores, axis=1, keepdims=True)
    for score_u in fresh:
        top = jnp.maximum(top, score_u)
    exp_cache = jnp.exp(scores - top)
    exp_fresh = [jnp.exp(score_u - top) for score_u in fresh]
    total = jnp.sum(exp_cache, axis=1, keepdims=True)
    for exp_u in exp_fresh:
        total = total + exp_u
    weights = (exp_cache / total).astype(jnp.bfloat16)
    both = jnp.dot(weights, values, preferred_element_type=jnp.float32)
    mixed = jnp.where(first_kv, both[:, :HD], both[:, HD:])
    for u in range(STEPS):
        value_u = jnp.where(first_kv, extra[4 + 2 * u : 5 + 2 * u], extra[5 + 2 * u : 6 + 2 * u])
        weight_u = (exp_fresh[u] / total).astype(jnp.bfloat16).astype(jnp.float32)
        mixed = mixed + weight_u * value_u
    return mixed


def each(count, body):
    if count <= 8:
        for i in range(count):
            body(i)
    else:
        pl.loop(0, count)(body)


def kernel(
    G, X, R, moves, stride,
    meta, pay, perm, keys_hbm, values_hbm, weight_hbm, out,
    keys, values, weight, qsend, qrecv, att, gath, part, mixed, peer, ready, got,
    load_sem, qs, qr, zs, zr, xs, xr, ts, tr, cs, cr, fs, fr,
):
    Z = G // X
    half = R // 2
    stays = R - moves
    cols = weight.shape[1]
    me = lax.axis_index("dp")
    core = lax.axis_index("tp")
    zi, xi = me // X, me % X
    side = (core + G - me) % 2

    loads = [
        pltpu.make_async_copy(keys_hbm, keys, load_sem.at[0]),
        pltpu.make_async_copy(values_hbm, values, load_sem.at[1]),
        pltpu.make_async_copy(weight_hbm, weight, load_sem.at[2]),
    ]
    for load in loads:
        load.start()

    barrier = pltpu.get_barrier_semaphore()
    for d in range(1, G):
        pl.semaphore_signal(
            barrier, inc=1, device_id={"dp": (me + d) % G}, device_id_type=MESH
        )
    pl.semaphore_signal(barrier, inc=1, device_id={"tp": 1 - core}, device_id_type=MESH)

    for k in range(moves):
        qsend[k] = pay[meta[stays + k]]
    pl.semaphore_wait(barrier, G)

    def remote(src, dst, send, recv, target):
        return pltpu.make_async_remote_copy(
            src_ref=src, dst_ref=dst, send_sem=send, recv_sem=recv,
            device_id=target, device_id_type=MESH,
        )

    q_copies = []
    for k in range(moves):
        off = 1 + k * stride
        copy = remote(
            qsend.at[k], qrecv.at[k], qs.at[k], qr.at[k], {"dp": (me + G - off) % G}
        )
        copy.start()
        q_copies.append(copy)
    loads[0].wait()
    loads[1].wait()

    def attend_piece(p):
        for j in range(half):
            m = p * half + j
            source = pay[meta[m]] if m < stays else qrecv[m - stays]
            row = meta[m]
            att[p, pl.ds(j * 32, 32), :] = attend_slot(
                source, keys[row], values[row], meta[R + m]
            )
        for h in range(16):
            gath[p, me, :, pl.ds(h * HD, HD)] = att[
                p, pl.ds(h, 2 * half, stride=16), :
            ].astype(jnp.bfloat16)

    def z_copy(p, d):
        return remote(
            gath.at[p, me], gath.at[p, me], zs.at[p, d - 1], zr.at[p, d - 1],
            {"dp": ((zi + d) % Z) * X + xi},
        )

    def x_copy(p, dx, d):
        block = ((zi + Z - d) % Z) * X + xi
        return remote(
            gath.at[p, block], gath.at[p, block], xs.at[p, dx - 1, d], xr.at[p, dx - 1, d],
            {"dp": zi * X + (xi + dx) % X},
        )

    def send_own(p):
        for dx in range(1, X):
            x_copy(p, dx, 0).start()
        for d in range(1, Z):
            z_copy(p, d).start()

    def forward(p):
        for d in range(1, Z):
            z_copy(p, d).wait_recv()
            for dx in range(1, X):
                x_copy(p, dx, d).start()

    attend_piece(0)
    send_own(0)
    for copy in q_copies:
        copy.wait_recv()
    attend_piece(1)
    send_own(1)
    forward(0)

    def project(p):
        for dx in range(1, X):
            for d in range(Z):
                x_copy(p, dx, d).wait_recv()
        block = min(G, 8)

        def rows(b):
            lhs = gath[p, pl.ds(b * block, block)].reshape(block * 16, weight.shape[0])
            res = jnp.dot(lhs, weight[...], preferred_element_type=jnp.float32)
            part[p, pl.ds(b * block, block)] = res.reshape(block, 16, cols)

        each(G // block, rows)

        def regroup(g):
            if p == 0:
                mixed[p, g % 2, g // 2] = part[p, g]
                return
            low = lax.broadcasted_iota(jnp.int32, (8, cols), 0) // 2
            for tile in range(2):
                acc = None
                for q in range(4):
                    m = half + tile * 4 + q
                    off = 0 if m < stays else 1 + (m - stays) * stride
                    val = part[p, (g + G - off) % G, pl.ds(tile * 8, 8), :]
                    acc = val if acc is None else jnp.where(low == q, val, acc)
                mixed[p, g % 2, g // 2, pl.ds(tile * 8, 8), :] = acc

        each(G, regroup)
        t_copy(p).start()

    def t_copy(p):
        return remote(
            mixed.at[p, 1 - core], peer.at[p], ts.at[p], tr.at[p], {"tp": 1 - core}
        )

    def c_copy(p, i):
        dist = 2 * i + side
        target = (me + dist) % G
        return remote(
            ready.at[p, target // 2], got.at[p, me], cs.at[p, i], cr.at[p, dist],
            {"dp": target},
        )

    def f_copy(p, dist):
        block = (me + G - dist) % G
        return remote(
            got.at[p, block], got.at[p, block], fs.at[p, dist], fr.at[p, dist],
            {"tp": 1 - core},
        )

    def scatter(p):
        t_copy(p).wait_recv()

        def add(j):
            ready[p, j] = (mixed[p, core, j] + peer[p, j]).astype(jnp.bfloat16)

        each(G // 2, add)

        @pl.when(side == 0)
        def _():
            got[p, me] = ready[p, me // 2]
            f_copy(p, 0).start()

        @pl.when(side == 1)
        def _():
            c_copy(p, 0).start()

        for i in range(1, G // 2):
            c_copy(p, i).start()

    def collect(p):
        @pl.when(side == 0)
        def _():
            for dist in range(1, G):
                remote(
                    ready.at[p, 0], got.at[p, (me + G - dist) % G], cs.at[p, dist // 2],
                    cr.at[p, dist], {"dp": (me + dist) % G},
                ).wait_recv()
                f_copy(p, dist).start()

        @pl.when(side == 1)
        def _():
            for dist in range(G):
                block = (me + G - dist) % G
                remote(
                    got.at[p, block], got.at[p, block], fs.at[p, dist], fr.at[p, dist],
                    {"tp": 1 - core},
                ).wait_recv()

    loads[2].wait()
    project(0)
    forward(1)
    scatter(0)
    project(1)
    scatter(1)
    collect(0)
    collect(1)

    def finish(g):
        both = jnp.concatenate([got[0, g], got[1, g]], axis=0)
        res = jnp.dot(perm[...], both, preferred_element_type=jnp.float32).astype(jnp.bfloat16)
        if cols % 128 == 0:
            out[:, pl.ds(g * cols, cols)] = res
        else:
            out[g] = res

    each(G, finish)

    for copy in q_copies:
        copy.wait_send()
    for p in range(2):
        for d in range(1, Z):
            z_copy(p, d).wait_send()
        for dx in range(1, X):
            for d in range(Z):
                x_copy(p, dx, d).wait_send()
        t_copy(p).wait_send()
        for i in range(1, G // 2):
            c_copy(p, i).wait_send()

        @pl.when(side == 1)
        def _():
            c_copy(p, 0).wait_send()

        @pl.when(side == 0)
        def _():
            for dist in range(G):
                f_copy(p, dist).wait_send()


def local(cache_keys, cache_values, lengths, move_to, queries, new_keys, new_values, out_weight):
    G = lax.axis_size("dp")
    R = lengths.shape[0]
    X = 2 if G <= 16 else 4
    moves = min(R // 2, G - 1)
    stride = max(1, G // (moves + 1))
    depth, cols = out_weight.shape
    me = lax.axis_index("dp")
    ids = jnp.arange(R, dtype=jnp.int32)
    off = (move_to // R + G - me) % G
    order = jnp.where(off == 0, ids, R + off)
    rank = jnp.sum((order[None, :] < order[:, None]).astype(jnp.int32), axis=1)
    hit = rank[None, :] == ids[:, None]
    index = jnp.sum(jnp.where(hit, ids[None, :], 0), axis=1)
    length = jnp.sum(jnp.where(hit, lengths[None, :], 0), axis=1)
    meta = jnp.concatenate([index, length])
    both_ids = jnp.arange(2 * R, dtype=jnp.int32)
    home = jnp.repeat(rank, 2) * 2 + both_ids % 2
    perm = (home[:, None] == both_ids[None, :]).astype(jnp.bfloat16)
    pay = jnp.concatenate(
        [
            queries.reshape(R, 32, HD),
            new_keys.reshape(R, 4, HD),
            new_values.reshape(R, 4, HD),
            jnp.zeros((R, PAY - 40, HD), jnp.bfloat16),
        ],
        axis=1,
    )
    wide = cols % 128 == 0
    out_shape = (2 * R, G * cols) if wide else (G, 2 * R, cols)
    dma = pltpu.SemaphoreType.DMA
    Z = G // X
    vmem = pl.BlockSpec(memory_space=pltpu.VMEM)
    anywhere = pl.BlockSpec(memory_space=pl.ANY)
    result = pl.pallas_call(
        functools.partial(kernel, G, X, R, moves, stride),
        out_shape=jax.ShapeDtypeStruct(out_shape, jnp.bfloat16),
        in_specs=[pl.BlockSpec(memory_space=pltpu.SMEM), vmem, vmem, anywhere, anywhere, anywhere],
        out_specs=vmem,
        scratch_shapes=[
            pltpu.VMEM(cache_keys.shape, jnp.bfloat16),
            pltpu.VMEM(cache_values.shape, jnp.bfloat16),
            pltpu.VMEM(out_weight.shape, jnp.bfloat16),
            pltpu.VMEM((moves, PAY, HD), jnp.bfloat16),
            pltpu.VMEM((moves, PAY, HD), jnp.bfloat16),
            pltpu.VMEM((2, R * 16, HD), jnp.float32),
            pltpu.VMEM((2, G, R, depth), jnp.bfloat16),
            pltpu.VMEM((2, G, R, cols), jnp.float32),
            pltpu.VMEM((2, 2, G // 2, R, cols), jnp.float32),
            pltpu.VMEM((2, G // 2, R, cols), jnp.float32),
            pltpu.VMEM((2, G // 2, R, cols), jnp.bfloat16),
            pltpu.VMEM((2, G, R, cols), jnp.bfloat16),
            dma((3,)),
            dma((moves,)),
            dma((moves,)),
            dma((2, Z - 1)),
            dma((2, Z - 1)),
            dma((2, X - 1, Z)),
            dma((2, X - 1, Z)),
            dma((2,)),
            dma((2,)),
            dma((2, G // 2)),
            dma((2, G)),
            dma((2, G)),
            dma((2, G)),
        ],
        compiler_params=pltpu.CompilerParams(
            collective_id=0, has_side_effects=True, vmem_limit_bytes=48 * 1024 * 1024
        ),
    )(meta, pay, perm, cache_keys, cache_values, out_weight)
    if not wide:
        result = jnp.transpose(result, (1, 0, 2))
    return result.reshape(R, STEPS, G * cols)


def solution(mesh):
    placed = (
        P(("parts", "dp"), None, "tp"),
        P(("parts", "dp"), None, "tp"),
        P(("parts", "dp")),
        P(("parts", "dp")),
        P(("parts", "dp"), None, "tp"),
        P(("parts", "dp"), None, "tp"),
        P(("parts", "dp"), None, "tp"),
        P("tp", "dp"),
    )
    return jax.shard_map(
        local, mesh=mesh, in_specs=placed, out_specs=P(("parts", "dp"), None, None), check_vma=False
    )
```

```python
import functools
import math

import jax
import jax.numpy as jnp
from jax import lax
from jax.experimental import pallas as pl
from jax.experimental.pallas import tpu as pltpu
from jax.sharding import PartitionSpec as P

KVH = 4
HD = 128
BLK = 128
STEPS = 2
PAY = 48
MESH = pl.DeviceIdType.MESH


def attend_slot(query, extra, keys, values, length):
    row = lax.broadcasted_iota(jnp.int32, (32, HD), 0)
    first_kv = (row // 8) % 2 == 0
    zero = jnp.zeros_like(query)
    wide = jnp.concatenate(
        [jnp.where(first_kv, query, zero), jnp.where(first_kv, zero, query)], axis=1
    ).astype(jnp.bfloat16)
    scale = 1.0 / math.sqrt(HD)
    scores = (
        lax.dot_general(wide, keys, (((1,), (1,)), ((), ())), preferred_element_type=jnp.float32)
        * scale
    )
    span = lax.broadcasted_iota(jnp.int32, scores.shape, 1)
    scores = jnp.where(span < length * BLK, scores, -jnp.inf)
    step = lax.broadcasted_iota(jnp.int32, (32, 1), 0) // 16
    fresh = []
    for u in range(STEPS):
        key_u = jnp.where(first_kv, extra[u : u + 1], extra[2 + u : 3 + u])
        score_u = jnp.sum(query * key_u, axis=1, keepdims=True) * scale
        fresh.append(jnp.where(step >= u, score_u, -jnp.inf))
    top = jnp.max(scores, axis=1, keepdims=True)
    for score_u in fresh:
        top = jnp.maximum(top, score_u)
    exp_cache = jnp.exp(scores - top)
    exp_fresh = [jnp.exp(score_u - top) for score_u in fresh]
    total = jnp.sum(exp_cache, axis=1, keepdims=True)
    for exp_u in exp_fresh:
        total = total + exp_u
    weights = (exp_cache / total).astype(jnp.bfloat16)
    both = jnp.dot(weights, values, preferred_element_type=jnp.float32)
    mixed = jnp.where(first_kv, both[:, :HD], both[:, HD:])
    for u in range(STEPS):
        value_u = jnp.where(first_kv, extra[4 + u : 5 + u], extra[6 + u : 7 + u])
        weight_u = (exp_fresh[u] / total).astype(jnp.bfloat16).astype(jnp.float32)
        mixed = mixed + weight_u * value_u
    return mixed


def equal(a, b):
    return 1 - jnp.minimum(jnp.maximum(a - b, b - a), 1)


def each(count, body):
    if count <= 8:
        for i in range(count):
            body(i)
    else:
        pl.loop(0, count)(body)


def kernel(
    G, X, R, moves, stride,
    move_to, lengths, queries, new_keys, new_values, keys_hbm, values_hbm, weight_hbm, out,
    keys, values, weight, qall, qrow, qsend, qrecv, att, gath, part, mixed, peer, ready, got,
    load_sem, qs, qr, zs, zr, xs, xr, ts, tr, cs, cr, fs, fr,
):
    Z = G // X
    half = R // 2
    stays = R - moves
    cols = weight.shape[1]
    me = lax.axis_index("dp")
    core = lax.axis_index("tp")
    zi, xi = me // X, me % X
    side = (core + G - me) % 2

    loads = [
        pltpu.make_async_copy(keys_hbm, keys, load_sem.at[0]),
        pltpu.make_async_copy(values_hbm, values, load_sem.at[1]),
        pltpu.make_async_copy(weight_hbm, weight, load_sem.at[2]),
    ]
    for load in loads:
        load.start()

    barrier = pltpu.get_barrier_semaphore()
    for d in range(1, G):
        pl.semaphore_signal(
            barrier, inc=1, device_id={"dp": (me + d) % G}, device_id_type=MESH
        )
    pl.semaphore_signal(barrier, inc=1, device_id={"tp": 1 - core}, device_id_type=MESH)

    offs = [lax.rem(lax.div(move_to[i], R) + G - me, G) for i in range(R)]
    index = [jnp.int32(0)] * R
    seen = jnp.int32(0)
    for i in range(R):
        leaves = jnp.minimum(offs[i], 1)
        slot = (1 - leaves) * seen + leaves * (stays + lax.div(offs[i] + stride - 1, stride) - 1)
        seen = seen + 1 - leaves
        index = [index[m] + i * equal(slot, m) for m in range(R)]
    index = [jnp.minimum(row, R - 1) for row in index]

    flat = queries[...].astype(jnp.float32).reshape(2 * R, 16 * HD)
    for h in range(16):
        qall[pl.ds(h, 2 * R, stride=16), :] = flat[:, h * HD : (h + 1) * HD]
    for i in range(R):
        qrow[i] = qall[i * 32 : i * 32 + 32, :].astype(jnp.bfloat16)

    def own_query(row):
        return qrow[row].astype(jnp.float32)

    def own_extra(row):
        key = new_keys[row].astype(jnp.float32)
        value = new_values[row].astype(jnp.float32)
        return jnp.concatenate(
            [key[:, :HD], key[:, HD:], value[:, :HD], value[:, HD:]], axis=0
        )

    for k in range(moves):
        row = index[stays + k]
        qsend[k, 0:32] = qrow[row]
        qsend[k, 32:48] = jnp.concatenate(
            [own_extra(row), jnp.zeros((8, HD), jnp.float32)], axis=0
        ).astype(jnp.bfloat16)
    pl.semaphore_wait(barrier, G)

    def remote(src, dst, send, recv, target):
        return pltpu.make_async_remote_copy(
            src_ref=src, dst_ref=dst, send_sem=send, recv_sem=recv,
            device_id=target, device_id_type=MESH,
        )

    q_copies = []
    for k in range(moves):
        off = 1 + k * stride
        copy = remote(
            qsend.at[k], qrecv.at[k], qs.at[k], qr.at[k], {"dp": (me + G - off) % G}
        )
        copy.start()
        q_copies.append(copy)
    loads[0].wait()
    loads[1].wait()

    def attend_piece(p):
        for j in range(half):
            m = p * half + j
            row = index[m]
            if m < stays:
                query, extra = own_query(row), own_extra(row)
            else:
                query = qrecv[m - stays, 0:32].astype(jnp.float32)
                extra = qrecv[m - stays, 32:48].astype(jnp.float32)
            att[p, pl.ds(j * 32, 32), :] = attend_slot(
                query, extra, keys[row], values[row], lengths[row]
            )
        for h in range(16):
            gath[p, me, :, pl.ds(h * HD, HD)] = att[
                p, pl.ds(h, 2 * half, stride=16), :
            ].astype(jnp.bfloat16)

    def z_copy(p, d):
        return remote(
            gath.at[p, me], gath.at[p, me], zs.at[p, d - 1], zr.at[p, d - 1],
            {"dp": ((zi + d) % Z) * X + xi},
        )

    def x_copy(p, dx, d):
        block = ((zi + Z - d) % Z) * X + xi
        return remote(
            gath.at[p, block], gath.at[p, block], xs.at[p, dx - 1, d], xr.at[p, dx - 1, d],
            {"dp": zi * X + (xi + dx) % X},
        )

    def send_own(p):
        for dx in range(1, X):
            x_copy(p, dx, 0).start()
        for d in range(1, Z):
            z_copy(p, d).start()

    def forward(p, first, last):
        for d in range(first, last):
            z_copy(p, d).wait_recv()
            for dx in range(1, X):
                x_copy(p, dx, d).start()

    attend_piece(0)
    send_own(0)
    for copy in q_copies:
        copy.wait_recv()
    attend_piece(1)
    send_own(1)
    forward(0, 1, Z)
    forward(1, 1, Z // 2)

    def project(p):
        for dx in range(1, X):
            for d in range(Z):
                x_copy(p, dx, d).wait_recv()
        block = min(G, 8)

        def rows(b):
            lhs = gath[p, pl.ds(b * block, block)].reshape(block * 16, weight.shape[0])
            res = jnp.dot(lhs, weight[...], preferred_element_type=jnp.float32)
            part[p, pl.ds(b * block, block)] = res.reshape(block, 16, cols)

        each(G // block, rows)

        def regroup(g):
            if p == 0:
                mixed[p, g % 2, g // 2] = part[p, g]
                return
            low = lax.broadcasted_iota(jnp.int32, (8, cols), 0) // 2
            for tile in range(2):
                acc = None
                for q in range(4):
                    m = half + tile * 4 + q
                    off = 0 if m < stays else 1 + (m - stays) * stride
                    val = part[p, (g + G - off) % G, pl.ds(tile * 8, 8), :]
                    acc = val if acc is None else jnp.where(low == q, val, acc)
                mixed[p, g % 2, g // 2, pl.ds(tile * 8, 8), :] = acc

        each(G, regroup)
        t_copy(p).start()

    def t_copy(p):
        return remote(
            mixed.at[p, 1 - core], peer.at[p], ts.at[p], tr.at[p], {"tp": 1 - core}
        )

    def c_copy(p, i):
        dist = 2 * i + side
        target = (me + dist) % G
        return remote(
            ready.at[p, target // 2], got.at[p, me], cs.at[p, i], cr.at[p, dist],
            {"dp": target},
        )

    def f_copy(p, dist):
        block = (me + G - dist) % G
        return remote(
            got.at[p, block], got.at[p, block], fs.at[p, dist], fr.at[p, dist],
            {"tp": 1 - core},
        )

    def scatter(p):
        t_copy(p).wait_recv()

        def add(j):
            ready[p, j] = (mixed[p, core, j] + peer[p, j]).astype(jnp.bfloat16)

        each(G // 2, add)

        @pl.when(side == 0)
        def _():
            got[p, me] = ready[p, me // 2]
            f_copy(p, 0).start()

        @pl.when(side == 1)
        def _():
            c_copy(p, 0).start()

        for i in range(1, G // 2):
            c_copy(p, i).start()

    def collect(p):
        @pl.when(side == 0)
        def _():
            for dist in range(1, G):
                remote(
                    ready.at[p, 0], got.at[p, (me + G - dist) % G], cs.at[p, dist // 2],
                    cr.at[p, dist], {"dp": (me + dist) % G},
                ).wait_recv()
                f_copy(p, dist).start()

        @pl.when(side == 1)
        def _():
            for dist in range(G):
                block = (me + G - dist) % G
                remote(
                    got.at[p, block], got.at[p, block], fs.at[p, dist], fr.at[p, dist],
                    {"tp": 1 - core},
                ).wait_recv()

    loads[2].wait()
    project(0)
    forward(1, Z // 2, Z)
    scatter(0)
    project(1)
    scatter(1)
    collect(0)
    collect(1)

    to_row = lax.broadcasted_iota(jnp.int32, (2 * R, 2 * R), 0)
    from_row = lax.broadcasted_iota(jnp.int32, (2 * R, 2 * R), 1)
    held = jnp.zeros((2 * R, 2 * R), jnp.int32)
    for m in range(R):
        held = jnp.where(from_row // 2 == m, index[m], held)
    perm = equal(held * 2 + from_row % 2, to_row).astype(jnp.float32).astype(jnp.bfloat16)

    def finish(g):
        both = jnp.concatenate([got[0, g], got[1, g]], axis=0)
        res = jnp.dot(perm, both, preferred_element_type=jnp.float32)
        if cols % 128 == 0:
            out[:, :, pl.ds(g * cols, cols)] = res.reshape(R, STEPS, cols).astype(jnp.bfloat16)
        else:
            out[g] = res.astype(jnp.bfloat16)

    each(G, finish)

    for copy in q_copies:
        copy.wait_send()
    for p in range(2):
        for d in range(1, Z):
            z_copy(p, d).wait_send()
        for dx in range(1, X):
            for d in range(Z):
                x_copy(p, dx, d).wait_send()
        t_copy(p).wait_send()
        for i in range(1, G // 2):
            c_copy(p, i).wait_send()

        @pl.when(side == 1)
        def _():
            c_copy(p, 0).wait_send()

        @pl.when(side == 0)
        def _():
            for dist in range(G):
                f_copy(p, dist).wait_send()


def local(cache_keys, cache_values, lengths, move_to, queries, new_keys, new_values, out_weight):
    G = lax.axis_size("dp")
    R = lengths.shape[0]
    X = 2 if G <= 16 else 4
    moves = min(R // 2, G - 1)
    stride = max(1, G // (moves + 1))
    depth, cols = out_weight.shape
    wide = cols % 128 == 0
    out_shape = (R, STEPS, G * cols) if wide else (G, 2 * R, cols)
    dma = pltpu.SemaphoreType.DMA
    Z = G // X
    smem = pl.BlockSpec(memory_space=pltpu.SMEM)
    vmem = pl.BlockSpec(memory_space=pltpu.VMEM)
    anywhere = pl.BlockSpec(memory_space=pl.ANY)
    result = pl.pallas_call(
        functools.partial(kernel, G, X, R, moves, stride),
        out_shape=jax.ShapeDtypeStruct(out_shape, jnp.bfloat16),
        in_specs=[smem, smem, vmem, vmem, vmem, anywhere, anywhere, anywhere],
        out_specs=vmem,
        scratch_shapes=[
            pltpu.VMEM(cache_keys.shape, jnp.bfloat16),
            pltpu.VMEM(cache_values.shape, jnp.bfloat16),
            pltpu.VMEM(out_weight.shape, jnp.bfloat16),
            pltpu.VMEM((R * 32, HD), jnp.float32),
            pltpu.VMEM((R, 32, HD), jnp.bfloat16),
            pltpu.VMEM((moves, PAY, HD), jnp.bfloat16),
            pltpu.VMEM((moves, PAY, HD), jnp.bfloat16),
            pltpu.VMEM((2, R * 16, HD), jnp.float32),
            pltpu.VMEM((2, G, R, depth), jnp.bfloat16),
            pltpu.VMEM((2, G, R, cols), jnp.float32),
            pltpu.VMEM((2, 2, G // 2, R, cols), jnp.float32),
            pltpu.VMEM((2, G // 2, R, cols), jnp.float32),
            pltpu.VMEM((2, G // 2, R, cols), jnp.bfloat16),
            pltpu.VMEM((2, G, R, cols), jnp.bfloat16),
            dma((3,)),
            dma((moves,)),
            dma((moves,)),
            dma((2, Z - 1)),
            dma((2, Z - 1)),
            dma((2, X - 1, Z)),
            dma((2, X - 1, Z)),
            dma((2,)),
            dma((2,)),
            dma((2, G // 2)),
            dma((2, G)),
            dma((2, G)),
            dma((2, G)),
        ],
        compiler_params=pltpu.CompilerParams(
            collective_id=0, has_side_effects=True, vmem_limit_bytes=60 * 1024 * 1024
        ),
    )(move_to, lengths, queries, new_keys, new_values, cache_keys, cache_values, out_weight)
    if wide:
        return result
    return jnp.transpose(result, (1, 0, 2)).reshape(R, STEPS, G * cols)


def solution(mesh):
    placed = (
        P(("parts", "dp"), None, "tp"),
        P(("parts", "dp"), None, "tp"),
        P(("parts", "dp")),
        P(("parts", "dp")),
        P(("parts", "dp"), None, "tp"),
        P(("parts", "dp"), None, "tp"),
        P(("parts", "dp"), None, "tp"),
        P("tp", "dp"),
    )
    return jax.shard_map(
        local, mesh=mesh, in_specs=placed, out_specs=P(("parts", "dp"), None, None), check_vma=False
    )
```

```python
import functools
import math

import jax
import jax.numpy as jnp
from jax import lax
from jax.experimental import pallas as pl
from jax.experimental.pallas import tpu as pltpu
from jax.sharding import PartitionSpec as P

KVH = 4
HD = 128
BLK = 128
STEPS = 2
PAY = 48
MESH = pl.DeviceIdType.MESH


def attend_slot(query, extra, keys, values, length):
    row = lax.broadcasted_iota(jnp.int32, (32, HD), 0)
    first_kv = (row // 8) % 2 == 0
    zero = jnp.zeros_like(query)
    wide = jnp.concatenate(
        [jnp.where(first_kv, query, zero), jnp.where(first_kv, zero, query)], axis=1
    ).astype(jnp.bfloat16)
    scale = 1.0 / math.sqrt(HD)
    scores = (
        lax.dot_general(wide, keys, (((1,), (1,)), ((), ())), preferred_element_type=jnp.float32)
        * scale
    )
    span = lax.broadcasted_iota(jnp.int32, scores.shape, 1)
    scores = jnp.where(span < length * BLK, scores, -jnp.inf)
    step = lax.broadcasted_iota(jnp.int32, (32, 1), 0) // 16
    fresh = []
    for u in range(STEPS):
        key_u = jnp.where(first_kv, extra[u : u + 1], extra[2 + u : 3 + u])
        score_u = jnp.sum(query * key_u, axis=1, keepdims=True) * scale
        fresh.append(jnp.where(step >= u, score_u, -jnp.inf))
    top = jnp.max(scores, axis=1, keepdims=True)
    for score_u in fresh:
        top = jnp.maximum(top, score_u)
    exp_cache = jnp.exp(scores - top)
    exp_fresh = [jnp.exp(score_u - top) for score_u in fresh]
    total = jnp.sum(exp_cache, axis=1, keepdims=True)
    for exp_u in exp_fresh:
        total = total + exp_u
    weights = (exp_cache / total).astype(jnp.bfloat16)
    both = jnp.dot(weights, values, preferred_element_type=jnp.float32)
    mixed = jnp.where(first_kv, both[:, :HD], both[:, HD:])
    for u in range(STEPS):
        value_u = jnp.where(first_kv, extra[4 + u : 5 + u], extra[6 + u : 7 + u])
        weight_u = (exp_fresh[u] / total).astype(jnp.bfloat16).astype(jnp.float32)
        mixed = mixed + weight_u * value_u
    return mixed


def equal(a, b):
    return 1 - jnp.minimum(jnp.maximum(a - b, b - a), 1)


def each(count, body):
    if count <= 8:
        for i in range(count):
            body(i)
    else:
        pl.loop(0, count)(body)


def kernel(
    G, X, R, moves, stride,
    move_to, lengths, queries, new_keys, new_values, keys_hbm, values_hbm, weight_hbm, out,
    keys, values, weight, qall, qrow, qsend, qrecv, att, gath, part, mixed, peer, ready, got,
    load_sem, qs, qr, zs, zr, xs, xr, ts, tr, cs, cr, fs, fr,
):
    Z = G // X
    half = R // 2
    stays = R - moves
    cols = weight.shape[1]
    me = lax.axis_index("dp")
    core = lax.axis_index("tp")
    zi, xi = me // X, me % X
    side = (core + G - me) % 2

    loads = [
        pltpu.make_async_copy(keys_hbm, keys, load_sem.at[0]),
        pltpu.make_async_copy(values_hbm, values, load_sem.at[1]),
        pltpu.make_async_copy(weight_hbm, weight, load_sem.at[2]),
    ]
    for load in loads:
        load.start()

    barrier = pltpu.get_barrier_semaphore()
    for d in range(1, G):
        pl.semaphore_signal(
            barrier, inc=1, device_id={"dp": (me + d) % G}, device_id_type=MESH
        )
    pl.semaphore_signal(barrier, inc=1, device_id={"tp": 1 - core}, device_id_type=MESH)

    offs = [lax.rem(lax.div(move_to[i], R) + G - me, G) for i in range(R)]
    index = [jnp.int32(0)] * R
    seen = jnp.int32(0)
    for i in range(R):
        leaves = jnp.minimum(offs[i], 1)
        slot = (1 - leaves) * seen + leaves * (stays + lax.div(offs[i] + stride - 1, stride) - 1)
        seen = seen + 1 - leaves
        index = [index[m] + i * equal(slot, m) for m in range(R)]
    index = [jnp.minimum(row, R - 1) for row in index]

    flat = queries[...].astype(jnp.float32).reshape(2 * R, 16 * HD)
    for h in range(16):
        qall[pl.ds(h, 2 * R, stride=16), :] = flat[:, h * HD : (h + 1) * HD]
    for i in range(R):
        qrow[i] = qall[i * 32 : i * 32 + 32, :].astype(jnp.bfloat16)

    def own_query(row):
        return qrow[row].astype(jnp.float32)

    def own_extra(row):
        key = new_keys[row].astype(jnp.float32)
        value = new_values[row].astype(jnp.float32)
        return jnp.concatenate(
            [key[:, :HD], key[:, HD:], value[:, :HD], value[:, HD:]], axis=0
        )

    for k in range(moves):
        row = index[stays + k]
        qsend[k, 0:32] = qrow[row]
        qsend[k, 32:48] = jnp.concatenate(
            [own_extra(row), jnp.zeros((8, HD), jnp.float32)], axis=0
        ).astype(jnp.bfloat16)
    pl.semaphore_wait(barrier, G)

    def remote(src, dst, send, recv, target):
        return pltpu.make_async_remote_copy(
            src_ref=src, dst_ref=dst, send_sem=send, recv_sem=recv,
            device_id=target, device_id_type=MESH,
        )

    q_copies = []
    for k in range(moves):
        off = 1 + k * stride
        copy = remote(
            qsend.at[k], qrecv.at[k], qs.at[k], qr.at[k], {"dp": (me + G - off) % G}
        )
        copy.start()
        q_copies.append(copy)
    loads[0].wait()
    loads[1].wait()

    def attend_piece(p):
        for j in range(half):
            m = p * half + j
            row = index[m]
            if m < stays:
                query, extra = own_query(row), own_extra(row)
            else:
                query = qrecv[m - stays, 0:32].astype(jnp.float32)
                extra = qrecv[m - stays, 32:48].astype(jnp.float32)
            att[p, pl.ds(j * 32, 32), :] = attend_slot(
                query, extra, keys[row], values[row], lengths[row]
            )
        for h in range(16):
            gath[p, me, :, pl.ds(h * HD, HD)] = att[
                p, pl.ds(h, 2 * half, stride=16), :
            ].astype(jnp.bfloat16)

    def z_copy(p, d):
        return remote(
            gath.at[p, me], gath.at[p, me], zs.at[p, d - 1], zr.at[p, d - 1],
            {"dp": ((zi + d) % Z) * X + xi},
        )

    def x_copy(p, dx, d):
        block = ((zi + Z - d) % Z) * X + xi
        return remote(
            gath.at[p, block], gath.at[p, block], xs.at[p, dx - 1, d], xr.at[p, dx - 1, d],
            {"dp": zi * X + (xi + dx) % X},
        )

    def send_own(p):
        z_copy(p, 1).start()
        for dx in range(1, X):
            x_copy(p, dx, 0).start()
        for d in range(2, Z):
            z_copy(p, d).start()

    def forward(p, first, last):
        for d in range(first, last):
            z_copy(p, d).wait_recv()
            for dx in range(1, X):
                x_copy(p, dx, d).start()

    attend_piece(0)
    send_own(0)
    for copy in q_copies:
        copy.wait_recv()
    attend_piece(1)
    send_own(1)
    forward(0, 1, Z)
    forward(1, 1, Z)

    def project(p):
        for dx in range(1, X):
            for d in range(Z):
                x_copy(p, dx, d).wait_recv()
        block = min(G, 8)

        def rows(b):
            lhs = gath[p, pl.ds(b * block, block)].reshape(block * 16, weight.shape[0])
            res = jnp.dot(lhs, weight[...], preferred_element_type=jnp.float32)
            part[p, pl.ds(b * block, block)] = res.reshape(block, 16, cols)

        each(G // block, rows)

        def regroup(g):
            if p == 0:
                mixed[p, g % 2, g // 2] = part[p, g]
                return
            low = lax.broadcasted_iota(jnp.int32, (8, cols), 0) // 2
            for tile in range(2):
                acc = None
                for q in range(4):
                    m = half + tile * 4 + q
                    off = 0 if m < stays else 1 + (m - stays) * stride
                    val = part[p, (g + G - off) % G, pl.ds(tile * 8, 8), :]
                    acc = val if acc is None else jnp.where(low == q, val, acc)
                mixed[p, g % 2, g // 2, pl.ds(tile * 8, 8), :] = acc

        each(G, regroup)
        t_copy(p).start()

    def t_copy(p):
        return remote(
            mixed.at[p, 1 - core], peer.at[p], ts.at[p], tr.at[p], {"tp": 1 - core}
        )

    def c_copy(p, i):
        dist = 2 * i + side
        target = (me + dist) % G
        return remote(
            ready.at[p, target // 2], got.at[p, me], cs.at[p, i], cr.at[p, dist],
            {"dp": target},
        )

    def f_copy(p, dist):
        block = (me + G - dist) % G
        return remote(
            got.at[p, block], got.at[p, block], fs.at[p, dist], fr.at[p, dist],
            {"tp": 1 - core},
        )

    def scatter(p):
        t_copy(p).wait_recv()

        def add(j):
            ready[p, j] = (mixed[p, core, j] + peer[p, j]).astype(jnp.bfloat16)

        each(G // 2, add)

        @pl.when(side == 0)
        def _():
            got[p, me] = ready[p, me // 2]
            f_copy(p, 0).start()

        @pl.when(side == 1)
        def _():
            c_copy(p, 0).start()

        for i in range(1, G // 2):
            c_copy(p, i).start()

    def collect(p):
        @pl.when(side == 0)
        def _():
            for dist in range(1, G):
                remote(
                    ready.at[p, 0], got.at[p, (me + G - dist) % G], cs.at[p, dist // 2],
                    cr.at[p, dist], {"dp": (me + dist) % G},
                ).wait_recv()
                f_copy(p, dist).start()

        @pl.when(side == 1)
        def _():
            for dist in range(G):
                block = (me + G - dist) % G
                remote(
                    got.at[p, block], got.at[p, block], fs.at[p, dist], fr.at[p, dist],
                    {"tp": 1 - core},
                ).wait_recv()

    loads[2].wait()
    project(0)
    scatter(0)
    project(1)
    scatter(1)
    collect(0)
    collect(1)

    to_row = lax.broadcasted_iota(jnp.int32, (2 * R, 2 * R), 0)
    from_row = lax.broadcasted_iota(jnp.int32, (2 * R, 2 * R), 1)
    held = jnp.zeros((2 * R, 2 * R), jnp.int32)
    for m in range(R):
        held = jnp.where(from_row // 2 == m, index[m], held)
    perm = equal(held * 2 + from_row % 2, to_row).astype(jnp.float32).astype(jnp.bfloat16)

    def finish(g):
        both = jnp.concatenate([got[0, g], got[1, g]], axis=0)
        res = jnp.dot(perm, both, preferred_element_type=jnp.float32)
        if cols % 128 == 0:
            out[:, :, pl.ds(g * cols, cols)] = res.reshape(R, STEPS, cols).astype(jnp.bfloat16)
        else:
            out[g] = res.astype(jnp.bfloat16)

    each(G, finish)

    for copy in q_copies:
        copy.wait_send()
    for p in range(2):
        for d in range(1, Z):
            z_copy(p, d).wait_send()
        for dx in range(1, X):
            for d in range(Z):
                x_copy(p, dx, d).wait_send()
        t_copy(p).wait_send()
        for i in range(1, G // 2):
            c_copy(p, i).wait_send()

        @pl.when(side == 1)
        def _():
            c_copy(p, 0).wait_send()

        @pl.when(side == 0)
        def _():
            for dist in range(G):
                f_copy(p, dist).wait_send()


def local(cache_keys, cache_values, lengths, move_to, queries, new_keys, new_values, out_weight):
    G = lax.axis_size("dp")
    R = lengths.shape[0]
    X = 2 if G <= 16 else 4
    moves = min(R // 2, G - 1)
    stride = max(1, G // (moves + 1))
    depth, cols = out_weight.shape
    wide = cols % 128 == 0
    out_shape = (R, STEPS, G * cols) if wide else (G, 2 * R, cols)
    dma = pltpu.SemaphoreType.DMA
    Z = G // X
    smem = pl.BlockSpec(memory_space=pltpu.SMEM)
    vmem = pl.BlockSpec(memory_space=pltpu.VMEM)
    anywhere = pl.BlockSpec(memory_space=pl.ANY)
    result = pl.pallas_call(
        functools.partial(kernel, G, X, R, moves, stride),
        out_shape=jax.ShapeDtypeStruct(out_shape, jnp.bfloat16),
        in_specs=[smem, smem, vmem, vmem, vmem, anywhere, anywhere, anywhere],
        out_specs=vmem,
        scratch_shapes=[
            pltpu.VMEM(cache_keys.shape, jnp.bfloat16),
            pltpu.VMEM(cache_values.shape, jnp.bfloat16),
            pltpu.VMEM(out_weight.shape, jnp.bfloat16),
            pltpu.VMEM((R * 32, HD), jnp.float32),
            pltpu.VMEM((R, 32, HD), jnp.bfloat16),
            pltpu.VMEM((moves, PAY, HD), jnp.bfloat16),
            pltpu.VMEM((moves, PAY, HD), jnp.bfloat16),
            pltpu.VMEM((2, R * 16, HD), jnp.float32),
            pltpu.VMEM((2, G, R, depth), jnp.bfloat16),
            pltpu.VMEM((2, G, R, cols), jnp.float32),
            pltpu.VMEM((2, 2, G // 2, R, cols), jnp.float32),
            pltpu.VMEM((2, G // 2, R, cols), jnp.float32),
            pltpu.VMEM((2, G // 2, R, cols), jnp.bfloat16),
            pltpu.VMEM((2, G, R, cols), jnp.bfloat16),
            dma((3,)),
            dma((moves,)),
            dma((moves,)),
            dma((2, Z - 1)),
            dma((2, Z - 1)),
            dma((2, X - 1, Z)),
            dma((2, X - 1, Z)),
            dma((2,)),
            dma((2,)),
            dma((2, G // 2)),
            dma((2, G)),
            dma((2, G)),
            dma((2, G)),
        ],
        compiler_params=pltpu.CompilerParams(
            collective_id=0, has_side_effects=True, vmem_limit_bytes=60 * 1024 * 1024
        ),
    )(move_to, lengths, queries, new_keys, new_values, cache_keys, cache_values, out_weight)
    if wide:
        return result
    return jnp.transpose(result, (1, 0, 2)).reshape(R, STEPS, G * cols)


def solution(mesh):
    placed = (
        P(("parts", "dp"), None, "tp"),
        P(("parts", "dp"), None, "tp"),
        P(("parts", "dp")),
        P(("parts", "dp")),
        P(("parts", "dp"), None, "tp"),
        P(("parts", "dp"), None, "tp"),
        P(("parts", "dp"), None, "tp"),
        P("tp", "dp"),
    )
    return jax.shard_map(
        local, mesh=mesh, in_specs=placed, out_specs=P(("parts", "dp"), None, None), check_vma=False
    )
```
